256 devices in a mesh: mrow: 32 (over x_hi, z, core), mcol: 8 (over y, x_lo).
Axes of the slice: x: 4 (x_hi: 2, x_lo: 2; x = x_hi * 2 + x_lo), y: 4, z: 8, core: 2. Of those that a mesh axis runs over, the one named last changes fastest.
Arguments:
- queries: bfloat16 [4096, 4096], P('mrow', 'mcol'), may hold values from -6 to 6
- grad_out: bfloat16 [4096, 4096], P('mrow', 'mcol'), may hold values from -6 to 6
- attn_out: bfloat16 [4096, 4096], P('mrow', 'mcol'), may hold values from -2 to 2
- log_sum: float32 [4096, 32], P('mrow', 'mcol'), as said below
- memory_keys: bfloat16 [256, 128, 1024], P('mrow', 'mcol'), may hold values from -6 to 6
- memory_values: bfloat16 [256, 128, 1024], P('mrow', 'mcol'), may hold values from -6 to 6
Outputs:
- grad_queries: float32 [4096, 4096], P('mrow', 'mcol')
The draws below stay inside these ranges and needn't reach their ends.
Inputs may be any that keep to these rules, and one draw needn't show every extreme that they name: `log_sum`: each entry is the natural logarithm of 32768, plus 0 to 1.
All inputs are finite; a program needn't handle non-finite values.
Results may differ from the reference program's by a relative error of at most 0.0023.
Values may be sent and summed in bfloat16 or wider, within the bound.
A program may use at most 64 MiB of HBM per device.

```python
import math
import jax
import jax.numpy as jnp
from jax import lax

H = 32
KVH = 8
HD = 128
MR_DEV = 8
TOKENS = 4096
MROWS = 256
MCOLS = 128
N_MROW = 32


def draw_log_sum(key, part):
    key = jax.random.fold_in(key, 7)
    offset = math.log(MROWS * MCOLS)
    spread = jax.random.uniform(key, (TOKENS, H), jnp.float32)
    return offset + spread


def steps_of(own_key, dims, pieces, low, largest):
    level, own = 1.0, jax.random.fold_in(own_key, 6)
    for dim, parts in pieces:
        draws = jnp.exp(jax.random.uniform(jax.random.fold_in(own, dim), (parts,), jnp.float32, low / len(pieces), largest / len(pieces)))
        level = level * jnp.repeat(draws, dims[dim] // parts).reshape([-1 if axis == dim else 1 for axis in range(len(dims))])
    return level


def bell_draw(rng, dims, scale, bound, shards=(), kind=jnp.bfloat16):
    level = steps_of(rng, dims, shards, -0.22, 0.18) if shards else 1.0
    drawn = jax.random.normal(rng, dims, jnp.float32) * scale * level
    return jnp.minimum(jnp.maximum(drawn, -bound), bound).astype(kind)


def setup_inputs(seed: int = 0) -> dict:
    key_of = jax.random.split(jax.random.key(seed), 7)
    queries = bell_draw(key_of[0], (TOKENS, H * HD), 1.0, 6.0, ((0, 32), (1, 8)))
    grad_out = bell_draw(key_of[1], (TOKENS, H * HD), 2.0, 6.0, ((0, 32), (1, 8)))
    attn_out = bell_draw(key_of[2], (TOKENS, H * HD), 0.15, 2.0, ((0, 32), (1, 8)))
    log_sum = draw_log_sum(jax.random.fold_in(key_of[6], 71), 0)
    memory_keys = bell_draw(key_of[4], (MROWS, MCOLS, KVH * HD), 1.0, 6.0, ((0, 32), (1, 8)))
    memory_values = bell_draw(key_of[5], (MROWS, MCOLS, KVH * HD), 2.0, 6.0, ((0, 32), (1, 8)))
    return {"queries": queries, "grad_out": grad_out, "attn_out": attn_out, "log_sum": log_sum, "memory_keys": memory_keys, "memory_values": memory_values}


def head_term(query_group, grad_group, log_group, dot_group, key_block, value_block):
    scaling = HD ** -0.5
    key_float = key_block.astype(jnp.float32)
    scores = jnp.einsum('tgd,ed->gte', query_group.astype(jnp.float32), key_float) * scaling
    weights = jnp.exp(scores - log_group[:, :, None])
    grad_probs = jnp.einsum('tgd,ed->gte', grad_group.astype(jnp.float32), value_block.astype(jnp.float32))
    grad_scores = (weights * (grad_probs - dot_group[:, :, None])).astype(jnp.bfloat16)
    grad_scores = lax.optimization_barrier(grad_scores).astype(jnp.float32)
    return scaling * jnp.einsum('gte,ed->tgd', grad_scores, key_float)


def reference(queries, grad_out, attn_out, log_sum, memory_keys, memory_values):
    token_count = queries.shape[0]
    per_group = H // KVH
    out_dot = jnp.sum((grad_out.astype(jnp.float32) * attn_out.astype(jnp.float32)).reshape(token_count, H, HD), axis=-1)
    query_heads = queries.reshape(token_count, KVH, per_group, HD).transpose(1, 0, 2, 3)
    grad_heads = grad_out.reshape(token_count, KVH, per_group, HD).transpose(1, 0, 2, 3)
    log_heads = log_sum.reshape(token_count, KVH, per_group).transpose(1, 2, 0)
    dot_heads = out_dot.reshape(token_count, KVH, per_group).transpose(1, 2, 0)
    key_blocks = memory_keys.reshape(N_MROW, MR_DEV * MCOLS, KVH, HD).transpose(0, 2, 1, 3)
    value_blocks = memory_values.reshape(N_MROW, MR_DEV * MCOLS, KVH, HD).transpose(0, 2, 1, 3)

    def memory_block(running, blocks):
        key_block, value_block = blocks
        terms = lax.map(lambda inputs: head_term(*inputs), (query_heads, grad_heads, log_heads, dot_heads, key_block, value_block))
        return running + terms, None

    running = jnp.zeros((KVH, token_count, per_group, HD), jnp.float32)
    running, unused = lax.scan(memory_block, running, (key_blocks, value_blocks))
    return running.transpose(1, 0, 2, 3).reshape(token_count, H * HD)
```

```python
import jax
import jax.numpy as jnp
from jax import lax
from jax.experimental import pallas as pl
from jax.experimental.pallas import tpu as pltpu
from jax.sharding import PartitionSpec as P

H = 32
KVH = 8
HD = 128
SCALE = HD ** -0.5
LOG2E = 1.4426950408889634
ZN = 8
F32 = jnp.float32
BF16 = jnp.bfloat16
MESH = pl.DeviceIdType.MESH
NT = (((1,), (1,)), ((), ()))
NN = (((1,), (0,)), ((), ()))

UNITS = (
    ((0, 0), (1, 0)),
    ((0, 1), (0, 7)),
    ((0, 2), (0, 6)),
    ((0, 3), (0, 5)),
    ((0, 4), (1, 4)),
    ((1, 3), (1, 5)),
    ((1, 2), (1, 6)),
    ((1, 1), (1, 7)),
)
POS = {block: 2 * u + i for u, unit in enumerate(UNITS) for i, block in enumerate(unit)}
UP, DOWN = 0, 1
GATHER = {(UP, 0): (0, 1, 2, 3), (UP, 1): (0, 1, 2), (DOWN, 0): (0, 7, 6), (DOWN, 1): (0, 7, 6, 5)}
REDUCE = {(DOWN, 0): (4, 3, 2, 1), (DOWN, 1): (3, 2, 1), (UP, 0): (5, 6, 7), (UP, 1): (4, 5, 6, 7)}
MESSAGES = [(d, hp, slot) for (d, hp), slots in REDUCE.items() for slot in slots]
MSG = {message: i for i, message in enumerate(MESSAGES)}
ROWS = 272
STEPS = 16


def kernel(
    l_ref, q_hbm, g_hbm, a_hbm, k_hbm, v_hbm, out_ref,
    qg, kv, kt, acc, abuf, sbuf, rbuf,
    local_sem, a2a_send, a2a_recv, fwd_send, fwd_recv, ring_send, ring_recv, red_send, red_recv,
):
    r, m = lax.axis_index("mrow"), lax.axis_index("mcol")
    xh, z, c = lax.div(r, 2 * ZN), lax.rem(lax.div(r, 2), ZN), lax.rem(r, 2)
    other = (1 - xh) * (2 * ZN) + z * 2 + c
    sibling = xh * (2 * ZN) + z * 2 + 1 - c
    above = xh * (2 * ZN) + lax.rem(z + 1, ZN) * 2 + c
    below = xh * (2 * ZN) + lax.rem(z + ZN - 1, ZN) * 2 + c
    toward = {UP: above, DOWN: below}

    def col(mr):
        return lax.rem(m + mr, KVH)

    def head_lanes(j):
        return pl.ds(pl.multiple_of(j * HD, HD), HD)

    local = []
    for hp in range(2):
        lanes = pl.ds(hp * 256, 256)
        local.append((q_hbm.at[:, lanes], qg.at[POS[hp, 0], pl.ds(0, 128)]))
        local.append((g_hbm.at[:, lanes], qg.at[POS[hp, 0], pl.ds(128, 128)]))
    local.append((a_hbm, abuf))
    local.append((k_hbm.at[:, head_lanes(m)], kv.at[0, 0]))
    local.append((v_hbm.at[:, head_lanes(m)], kv.at[1, 0]))
    local = [pltpu.make_async_copy(s, d, local_sem.at[i]) for i, (s, d) in enumerate(local)]
    for copy in local:
        copy.start()

    barrier = pltpu.get_barrier_semaphore()
    peers = [(r, col(mr)) for mr in range(1, KVH)] + [(other, col(mr)) for mr in range(KVH)]
    peers += [(sibling, m), (above, m), (below, m)]
    for peer in peers:
        pl.semaphore_signal(barrier, inc=1, device_id=peer, device_id_type=MESH)
    pl.semaphore_wait(barrier, len(peers))

    a2a = []
    for xr in range(2):
        for mr in range(1 - xr, KVH):
            for i, hbm in enumerate((k_hbm, v_hbm)):
                copy = pltpu.make_async_remote_copy(
                    src_ref=hbm.at[:, head_lanes(col(mr))],
                    dst_ref=kv.at[i, xr * 16 + (KVH - mr) % KVH],
                    send_sem=a2a_send.at[xr, i, mr],
                    recv_sem=a2a_recv.at[xr, i],
                    device_id=(other if xr else r, col(mr)),
                    device_id_type=MESH,
                )
                copy.start()
                a2a.append(copy)

    for copy in local[:5]:
        copy.wait()
    lane = lax.broadcasted_iota(jnp.int32, (128, 128), 1)
    stats = jnp.zeros((128, 128), F32)
    for h in range(4):
        hp, hl = h // 2, h % 2
        grad = qg[POS[hp, 0], 128:256, hl * 128 : hl * 128 + 128].astype(F32)
        attn = abuf[:, h * 128 : h * 128 + 128].astype(F32)
        stats = jnp.where(lane == h, l_ref[:, h : h + 1] * LOG2E, stats)
        stats = jnp.where(lane == 4 + h, jnp.sum(grad * attn, axis=1, keepdims=True), stats)
    stats = stats.T
    row = lax.broadcasted_iota(jnp.int32, (16, 256), 0)
    for hp in range(2):
        packed = jnp.zeros((16, 256), F32)
        for i in range(2):
            rest = jnp.concatenate([stats[4 * i + 2 * hp + hl : 4 * i + 2 * hp + hl + 1] for hl in range(2)], axis=1)
            for piece in range(3):
                part = rest.astype(BF16).astype(F32)
                packed = jnp.where(row == 3 * i + piece, part, packed)
                rest = rest - part
        qg[POS[hp, 0], 256:272, :] = packed.astype(BF16)

    def ring(d, hp, hop):
        slot = GATHER[d, hp][hop]
        landing = (slot + 1) % ZN if d == UP else (slot + ZN - 1) % ZN
        return pltpu.make_async_remote_copy(
            src_ref=qg.at[POS[hp, slot]],
            dst_ref=qg.at[POS[hp, landing]],
            send_sem=ring_send.at[d, hp, hop],
            recv_sem=ring_recv.at[d, hp, hop],
            device_id=(toward[d], m),
            device_id_type=MESH,
        )

    def pass_on(hp, hop):
        for d in (UP, DOWN):
            hops = len(GATHER[d, hp])
            if hop > 0 and hop <= hops:
                ring(d, hp, hop - 1).wait_recv()
            if hop < hops:
                ring(d, hp, hop).start()

    pass_on(0, 0)
    pass_on(1, 0)

    def forward(xr):
        return pltpu.make_async_remote_copy(
            src_ref=kv.at[:, pl.ds(xr * 16, 8)],
            dst_ref=kv.at[:, pl.ds(xr * 16 + 8, 8)],
            send_sem=fwd_send.at[xr],
            recv_sem=fwd_recv.at[xr],
            device_id=(sibling, m),
            device_id_type=MESH,
        )

    def send_forward(xr):
        for i in range(2):
            got = kv.at[i, pl.ds(xr * 16 + 1 - xr, 7 + xr)]
            pltpu.make_async_copy(got, got, a2a_recv.at[xr, i]).wait()
        forward(xr).start()

    def turn(first):
        def one(s, _):
            kt[first + s] = kv[0, first + s].T
            return 0

        lax.fori_loop(0, 8, one, 0)

    def take_forward(xr):
        turn(xr * 16)
        forward(xr).wait_recv()
        turn(xr * 16 + 8)

    def zero(i, _):
        acc[i] = jnp.zeros((128, 256), F32)
        return 0

    lax.fori_loop(0, 16, zero, 0)
    for copy in local[5:]:
        copy.wait()
    send_forward(0)
    pass_on(0, 1)
    take_forward(0)

    def reduce_copy(d, hp, slot):
        i = MSG[d, hp, slot]
        return pltpu.make_async_remote_copy(
            src_ref=sbuf.at[i],
            dst_ref=rbuf.at[i],
            send_sem=red_send.at[i],
            recv_sem=red_recv.at[i],
            device_id=(toward[d], m),
            device_id_type=MESH,
        )

    def send_sum(d, hp, slot):
        total = acc[POS[hp, slot]]
        before = (d, hp, slot + 1 if d == DOWN else slot - 1)
        if before in MSG:
            reduce_copy(*before).wait_recv()
            total = total + rbuf[MSG[before]].astype(F32)
        sbuf[MSG[d, hp, slot]] = total.astype(BF16)
        reduce_copy(d, hp, slot).start()

    def finish(hp):
        total = acc[POS[hp, 0]]
        for last in ((DOWN, hp, 1), (UP, hp, 7)):
            reduce_copy(*last).wait_recv()
            total = total + rbuf[MSG[last]].astype(F32)
        total = total * SCALE
        for hl in range(2):
            h = 2 * hp + hl
            out_ref[:, h * 128 : h * 128 + 128] = total[:, hl * 128 : hl * 128 + 128].T

    def work(u, half):
        first = half * 16
        ks = kv[0, pl.ds(first, 16)].reshape(16 * 128, HD)
        vs = kv[1, pl.ds(first, 16)].reshape(16 * 128, HD)
        blocks = [qg[2 * u], qg[2 * u + 1]]
        qs = jnp.concatenate([b[0:128, i : i + 128] for b in blocks for i in (0, 128)], axis=0)
        gs = jnp.concatenate([b[128:256, i : i + 128] for b in blocks for i in (0, 128)], axis=0)
        st = jnp.concatenate([b[256:272] for b in blocks], axis=1).astype(F32)
        logs = st[0:1] + st[1:2] + st[2:3]
        dots = st[3:4] + st[4:5] + st[5:6]
        scores = lax.dot_general(ks, qs, NT, preferred_element_type=F32)
        probs = lax.dot_general(vs, gs, NT, preferred_element_type=F32)
        ds = (jnp.exp2(scores * (SCALE * LOG2E) - logs) * (probs - dots)).astype(BF16)
        keys = jnp.concatenate([kt[first + i] for i in range(16)], axis=1)
        part = lax.dot_general(keys, ds, NN, preferred_element_type=F32)
        acc[2 * u] += part[:, :256]
        acc[2 * u + 1] += part[:, 256:]

    events = {
        0: [(pass_on, 1, 1)],
        1: [(pass_on, 0, 2), (send_forward, 1)],
        2: [(take_forward, 1), (pass_on, 1, 2)],
        4: [(pass_on, 0, 3)],
        5: [(pass_on, 1, 3)],
        7: [(pass_on, 0, 4), (pass_on, 1, 4), (send_sum, UP, 0, 5)],
        9: [(send_sum, DOWN, 0, 4), (send_sum, UP, 1, 4), (send_sum, UP, 0, 6)],
        11: [
            (send_sum, UP, 1, 5), (send_sum, DOWN, 0, 3), (send_sum, DOWN, 1, 3), (send_sum, UP, 0, 7),
        ],
        13: [(send_sum, UP, 1, 6), (send_sum, DOWN, 1, 2), (send_sum, DOWN, 0, 2)],
        14: [(send_sum, DOWN, 0, 1)],
        15: [(send_sum, UP, 1, 7), (send_sum, DOWN, 1, 1)],
    }

    def one_step(i, _):
        u = jnp.where(i < 3, i, jnp.where(i < 6, i - 3, lax.div(i, 2)))
        half = jnp.where(i < 3, 0, jnp.where(i < 6, 1, lax.rem(i, 2)))
        work(u, half)
        for when, calls in events.items():
            @pl.when(i == when)
            def _(calls=calls):
                for call in calls:
                    call[0](*call[1:])
        return 0

    lax.fori_loop(0, STEPS, one_step, 0)
    finish(0)
    finish(1)

    for copy in a2a:
        copy.wait_send()
    for xr in range(2):
        forward(xr).wait_send()
    for (d, hp), hops in GATHER.items():
        for hop in range(len(hops)):
            ring(d, hp, hop).wait_send()
    for message in MESSAGES:
        reduce_copy(*message).wait_send()


def body(queries, grad_out, attn_out, log_sum, memory_keys, memory_values):
    entries = memory_keys.shape[0] * memory_keys.shape[1]
    any_space = pl.BlockSpec(memory_space=pl.ANY)
    in_vmem = pl.BlockSpec(memory_space=pltpu.VMEM)
    return pl.pallas_call(
        kernel,
        out_shape=jax.ShapeDtypeStruct(queries.shape, F32),
        in_specs=[in_vmem] + [any_space] * 5,
        out_specs=in_vmem,
        scratch_shapes=[
            pltpu.VMEM((16, ROWS, 256), BF16),
            pltpu.VMEM((2, 32, 128, HD), BF16),
            pltpu.VMEM((32, HD, 128), BF16),
            pltpu.VMEM((16, HD, 256), F32),
            pltpu.VMEM((128, 512), BF16),
            pltpu.VMEM((len(MESSAGES), HD, 256), BF16),
            pltpu.VMEM((len(MESSAGES), HD, 256), BF16),
            pltpu.SemaphoreType.DMA((7,)),
            pltpu.SemaphoreType.DMA((2, 2, KVH)),
            pltpu.SemaphoreType.DMA((2, 2)),
            pltpu.SemaphoreType.DMA((2,)),
            pltpu.SemaphoreType.DMA((2,)),
            pltpu.SemaphoreType.DMA((2, 2, 4)),
            pltpu.SemaphoreType.DMA((2, 2, 4)),
            pltpu.SemaphoreType.DMA((len(MESSAGES),)),
            pltpu.SemaphoreType.DMA((len(MESSAGES),)),
        ],
        compiler_params=pltpu.CompilerParams(
            collective_id=0, has_side_effects=True, vmem_limit_bytes=60 << 20
        ),
        cost_estimate=pl.CostEstimate(flops=12884901888, bytes_accessed=2 << 20, transcendentals=16777216),
    )(
        log_sum,
        queries,
        grad_out,
        attn_out,
        memory_keys.reshape(entries, KVH * HD),
        memory_values.reshape(entries, KVH * HD),
    )


def solution(mesh):
    return jax.shard_map(
        body,
        mesh=mesh,
        in_specs=(
            P("mrow", "mcol"),
            P("mrow", "mcol"),
            P("mrow", "mcol"),
            P("mrow", "mcol"),
            P("mrow", "mcol", None),
            P("mrow", "mcol", None),
        ),
        out_specs=P("mrow", "mcol"),
        check_vma=False,
    )
```

```python
import jax
import jax.numpy as jnp
from jax import lax
from jax.experimental import pallas as pl
from jax.experimental.pallas import tpu as pltpu
from jax.sharding import PartitionSpec as P

H = 32
KVH = 8
HD = 128
SCALE = HD ** -0.5
LOG2E = 1.4426950408889634
ZN = 8
F32 = jnp.float32
BF16 = jnp.bfloat16
MESH = pl.DeviceIdType.MESH
NT = (((1,), (1,)), ((), ()))
NN = (((1,), (0,)), ((), ()))

UNITS = (
    ((0, 0), (1, 0)),
    ((0, 1), (0, 7)),
    ((1, 1), (1, 7)),
    ((0, 2), (0, 6)),
    ((1, 2), (1, 6)),
    ((0, 3), (0, 5)),
    ((1, 3), (1, 5)),
    ((0, 4), (1, 4)),
)
POS = {block: 2 * u + i for u, unit in enumerate(UNITS) for i, block in enumerate(unit)}
UP, DOWN, FAR = 0, 1, 2
GATHER = {(UP, 0): (0, 1, 2, 3), (UP, 1): (0, 1, 2), (DOWN, 0): (0, 7, 6), (DOWN, 1): (0, 7, 6, 5)}
REDUCE = {(DOWN, 0): (3, 2, 1), (DOWN, 1): (3, 2, 1), (UP, 0): (5, 6, 7), (UP, 1): (5, 6, 7), (FAR, 0): (4,), (FAR, 1): (4,)}
MESSAGES = [(d, hp, slot) for (d, hp), slots in REDUCE.items() for slot in slots]
MSG = {message: i for i, message in enumerate(MESSAGES)}
ROWS = 272
STEP_UNIT = (0, 1, 2, 3, 4, 5, 6, 5, 6, 3, 4, 7, 7, 1, 2, 0)
STEP_HALF = (0, 0, 0, 0, 0, 0, 0, 1, 1, 1, 1, 0, 1, 1, 1, 1)


def pick(i, table):
    value = table[-1]
    for k in reversed(range(len(table) - 1)):
        value = jnp.where(i <= k, table[k], value)
    return value


def kernel(
    q_hbm, g_hbm, a_hbm, l_hbm, k_hbm, v_hbm, out_ref,
    qg, kv, kt, acc, abuf, lbuf, sbuf, rbuf,
    local_sem, a2a_send, a2a_recv, relay_send, relay_recv, fwd_send, fwd_recv, ring_send, ring_recv, red_send, red_recv,
):
    r, m = lax.axis_index("mrow"), lax.axis_index("mcol")
    xh, z, c = lax.div(r, 2 * ZN), lax.rem(lax.div(r, 2), ZN), lax.rem(r, 2)
    other = (1 - xh) * (2 * ZN) + z * 2 + c
    sibling = xh * (2 * ZN) + z * 2 + 1 - c
    above = xh * (2 * ZN) + lax.rem(z + 1, ZN) * 2 + c
    below = xh * (2 * ZN) + lax.rem(z + ZN - 1, ZN) * 2 + c
    far = xh * (2 * ZN) + lax.rem(z + ZN // 2, ZN) * 2 + c
    toward = {UP: above, DOWN: below, FAR: far}

    def col(mr):
        return lax.rem(m + mr, KVH)

    def head_lanes(j):
        return pl.ds(pl.multiple_of(j * HD, HD), HD)

    local = []
    for i, hbm in enumerate((q_hbm, g_hbm)):
        for hp in range(2):
            lanes = pl.ds(hp * 256, 256)
            local.append((hbm.at[:, lanes], qg.at[POS[hp, 0], pl.ds(i * 128, 128)]))
    local.append((a_hbm, abuf))
    local.append((l_hbm, lbuf))
    local.append((k_hbm.at[:, head_lanes(m)], kv.at[0, 0]))
    local.append((v_hbm.at[:, head_lanes(m)], kv.at[1, 0]))
    local = [pltpu.make_async_copy(s, d, local_sem.at[i]) for i, (s, d) in enumerate(local)]
    for copy in local:
        copy.start()

    barrier = pltpu.get_barrier_semaphore()
    peers = [(r, col(mr)) for mr in range(1, KVH)]
    peers += [(other, m), (sibling, m), (above, m), (below, m), (far, m)]
    for peer in peers:
        pl.semaphore_signal(barrier, inc=1, device_id=peer, device_id_type=MESH)

    def a2a(mr, i):
        slot = KVH - mr
        return pltpu.make_async_remote_copy(
            src_ref=(k_hbm, v_hbm)[i].at[:, head_lanes(col(mr))],
            dst_ref=kv.at[i, slot],
            send_sem=a2a_send.at[i, mr],
            recv_sem=a2a_recv.at[slot // 4, i],
            device_id=(r, col(mr)),
            device_id_type=MESH,
        )

    def wait_a2a(g):
        for i in range(2):
            got = kv.at[i, pl.ds(4 * g + 1 - g, 3 + g)]
            pltpu.make_async_copy(got, got, a2a_recv.at[g, i]).wait()

    def relay(g):
        return pltpu.make_async_remote_copy(
            src_ref=kv.at[:, pl.ds(4 * g, 4)],
            dst_ref=kv.at[:, pl.ds(16 + 8 * g, 4)],
            send_sem=relay_send.at[g],
            recv_sem=relay_recv.at[g],
            device_id=(other, m),
            device_id_type=MESH,
        )

    def forward(xr, g):
        here, there = ((4 * g, 8 + 4 * g), (16 + 8 * g, 20 + 8 * g))[xr]
        return pltpu.make_async_remote_copy(
            src_ref=kv.at[:, pl.ds(here, 4)],
            dst_ref=kv.at[:, pl.ds(there, 4)],
            send_sem=fwd_send.at[xr, g],
            recv_sem=fwd_recv.at[xr, g],
            device_id=(sibling, m),
            device_id_type=MESH,
        )

    def turn(first, count):
        def one(s, _):
            kt[first + s] = kv[0, first + s].T
            return 0

        lax.fori_loop(0, count, one, 0)

    def start_forward(g):
        relay(g).wait_recv()
        forward(1, g).start()
        turn(16 + 8 * g, 4)

    def take_forward(g):
        forward(1, g).wait_recv()
        turn(20 + 8 * g, 4)

    def ring(d, hp, hop, part):
        slot = GATHER[d, hp][hop]
        landing = (slot + 1) % ZN if d == UP else (slot + ZN - 1) % ZN
        rows = pl.ds(0, ROWS)
        return pltpu.make_async_remote_copy(
            src_ref=qg.at[POS[hp, slot], rows],
            dst_ref=qg.at[POS[hp, landing], rows],
            send_sem=ring_send.at[d, hp, hop, part],
            recv_sem=ring_recv.at[d, hp, hop, part],
            device_id=(toward[d], m),
            device_id_type=MESH,
        )

    def pass_on(hp, hop, parts=(0,)):
        for part in parts:
            for d in (UP, DOWN):
                hops = len(GATHER[d, hp])
                if hop > 0 and hop <= hops:
                    ring(d, hp, hop - 1, part).wait_recv()
                if hop < hops:
                    ring(d, hp, hop, part).start()

    def zero(i, _):
        acc[i] = jnp.zeros((128, 256), F32)
        return 0

    for copy in local[:6]:
        copy.wait()

    lane = lax.broadcasted_iota(jnp.int32, (128, 128), 1)
    stats = jnp.zeros((128, 128), F32)
    for h in range(4):
        hp, hl = h // 2, h % 2
        grad = qg[POS[hp, 0], 128:256, hl * 128 : hl * 128 + 128].astype(F32)
        attn = abuf[:, h * 128 : h * 128 + 128].astype(F32)
        stats = jnp.where(lane == h, jnp.sum(grad * attn, axis=1, keepdims=True), stats)
    stats = stats.T
    row = lax.broadcasted_iota(jnp.int32, (16, 256), 0)
    stats = (lbuf[...] * LOG2E, stats)
    for hp in range(2):
        packed = jnp.zeros((16, 256), F32)
        for i in range(2):
            rest = jnp.concatenate([stats[i][2 * hp + hl : 2 * hp + hl + 1] for hl in range(2)], axis=1)
            for piece in range(3):
                part = rest.astype(BF16).astype(F32)
                packed = jnp.where(row == 3 * i + piece, part, packed)
                rest = rest - part
        qg[POS[hp, 0], 256:272, :] = packed.astype(BF16)

    pl.semaphore_wait(barrier, len(peers))
    pass_on(0, 0)
    for mr in reversed(range(1, KVH)):
        for i in range(2):
            a2a(mr, i).start()
    pass_on(1, 0)
    lax.fori_loop(0, 16, zero, 0)
    for copy in local[6:]:
        copy.wait()
    for g in range(2):
        wait_a2a(g)
        relay(g).start()
        forward(0, g).start()
        pass_on(g, 1)
    turn(0, 8)
    for g in range(2):
        forward(0, g).wait_recv()
    turn(8, 8)
    pass_on(0, 2)

    def reduce_copy(d, hp, slot):
        i = MSG[d, hp, slot]
        return pltpu.make_async_remote_copy(
            src_ref=sbuf.at[i],
            dst_ref=rbuf.at[i],
            send_sem=red_send.at[i],
            recv_sem=red_recv.at[i],
            device_id=(toward[d], m),
            device_id_type=MESH,
        )

    def send_sum(d, hp, slot):
        total = acc[POS[hp, slot]]
        before = (d, hp, slot + 1 if d == DOWN else slot - 1)
        if before in MSG and d != FAR:
            reduce_copy(*before).wait_recv()
            total = total + rbuf[MSG[before]].astype(F32)
        sbuf[MSG[d, hp, slot]] = total.astype(BF16)
        reduce_copy(d, hp, slot).start()

    def finish(hp):
        total = acc[POS[hp, 0]]
        for last in ((FAR, hp, 4), (DOWN, hp, 1), (UP, hp, 7)):
            reduce_copy(*last).wait_recv()
            total = total + rbuf[MSG[last]].astype(F32)
        total = total * SCALE
        for hl in range(2):
            h = 2 * hp + hl
            out_ref[:, h * 128 : h * 128 + 128] = total[:, hl * 128 : hl * 128 + 128].T

    def work(u, half):
        first = half * 16
        ks = kv[0, pl.ds(first, 16)].reshape(16 * 128, HD)
        vs = kv[1, pl.ds(first, 16)].reshape(16 * 128, HD)
        blocks = [qg[2 * u], qg[2 * u + 1]]
        qs = jnp.concatenate([b[0:128, i : i + 128] for b in blocks for i in (0, 128)], axis=0)
        gs = jnp.concatenate([b[128:256, i : i + 128] for b in blocks for i in (0, 128)], axis=0)
        st = jnp.concatenate([b[256:272] for b in blocks], axis=1).astype(F32)
        logs = st[0:1] + st[1:2] + st[2:3]
        dots = st[3:4] + st[4:5] + st[5:6]
        scores = lax.dot_general(ks, qs, NT, preferred_element_type=F32)
        probs = lax.dot_general(vs, gs, NT, preferred_element_type=F32)
        ds = (jnp.exp2(scores * (SCALE * LOG2E) - logs) * (probs - dots)).astype(BF16)
        keys = jnp.concatenate([kt[first + i] for i in range(16)], axis=1)
        part = lax.dot_general(keys, ds, NN, preferred_element_type=F32)
        acc[2 * u] += part[:, :256]
        acc[2 * u + 1] += part[:, 256:]

    events = {
        0: [(pass_on, 1, 2)],
        2: [(pass_on, 0, 3)],
        3: [(start_forward, 0)],
        4: [(pass_on, 1, 3)],
        5: [(start_forward, 1), (take_forward, 0)],
        6: [(take_forward, 1)],
        7: [(send_sum, UP, 0, 5), (send_sum, DOWN, 0, 3)],
        8: [(send_sum, UP, 1, 5), (send_sum, DOWN, 1, 3)],
        10: [(pass_on, 0, 4), (pass_on, 1, 4), (send_sum, UP, 0, 6), (send_sum, DOWN, 0, 2)],
        11: [(send_sum, UP, 1, 6), (send_sum, DOWN, 1, 2)],
        12: [(send_sum, FAR, 0, 4), (send_sum, FAR, 1, 4)],
        13: [(send_sum, UP, 0, 7), (send_sum, DOWN, 0, 1)],
        14: [(send_sum, UP, 1, 7), (send_sum, DOWN, 1, 1)],
    }

    def one_step(i, _):
        work(pick(i, STEP_UNIT), pick(i, STEP_HALF))
        for when, calls in events.items():
            @pl.when(i == when)
            def _(calls=calls):
                for call in calls:
                    call[0](*call[1:])
        return 0

    lax.fori_loop(0, len(STEP_UNIT), one_step, 0)
    finish(0)
    finish(1)

    for mr in range(1, KVH):
        for i in range(2):
            a2a(mr, i).wait_send()
    for g in range(2):
        relay(g).wait_send()
        for xr in range(2):
            forward(xr, g).wait_send()
    for (d, hp), hops in GATHER.items():
        for hop in range(len(hops)):
            for part in range(1):
                ring(d, hp, hop, part).wait_send()
    for message in MESSAGES:
        reduce_copy(*message).wait_send()


def body(queries, grad_out, attn_out, log_sum, memory_keys, memory_values):
    entries = memory_keys.shape[0] * memory_keys.shape[1]
    any_space = pl.BlockSpec(memory_space=pl.ANY)
    in_vmem = pl.BlockSpec(memory_space=pltpu.VMEM)
    return pl.pallas_call(
        kernel,
        out_shape=jax.ShapeDtypeStruct(queries.shape, F32),
        in_specs=[any_space] * 6,
        out_specs=in_vmem,
        scratch_shapes=[
            pltpu.VMEM((16, ROWS, 256), BF16),
            pltpu.VMEM((2, 32, 128, HD), BF16),
            pltpu.VMEM((32, HD, 128), BF16),
            pltpu.VMEM((16, HD, 256), F32),
            pltpu.VMEM((128, 512), BF16),
            pltpu.VMEM((4, 128), F32),
            pltpu.VMEM((len(MESSAGES), HD, 256), BF16),
            pltpu.VMEM((len(MESSAGES), HD, 256), BF16),
            pltpu.SemaphoreType.DMA((8,)),
            pltpu.SemaphoreType.DMA((2, KVH)),
            pltpu.SemaphoreType.DMA((2, 2)),
            pltpu.SemaphoreType.DMA((2,)),
            pltpu.SemaphoreType.DMA((2,)),
            pltpu.SemaphoreType.DMA((2, 2)),
            pltpu.SemaphoreType.DMA((2, 2)),
            pltpu.SemaphoreType.DMA((2, 2, 4, 2)),
            pltpu.SemaphoreType.DMA((2, 2, 4, 2)),
            pltpu.SemaphoreType.DMA((len(MESSAGES),)),
            pltpu.SemaphoreType.DMA((len(MESSAGES),)),
        ],
        compiler_params=pltpu.CompilerParams(
            collective_id=0, has_side_effects=True, vmem_limit_bytes=60 << 20
        ),
        cost_estimate=pl.CostEstimate(flops=12884901888, bytes_accessed=2 << 20, transcendentals=16777216),
    )(
        queries,
        grad_out,
        attn_out,
        log_sum.T,
        memory_keys.reshape(entries, KVH * HD),
        memory_values.reshape(entries, KVH * HD),
    )


def solution(mesh):
    return jax.shard_map(
        body,
        mesh=mesh,
        in_specs=(
            P("mrow", "mcol"),
            P("mrow", "mcol"),
            P("mrow", "mcol"),
            P("mrow", "mcol"),
            P("mrow", "mcol", None),
            P("mrow", "mcol", None),
        ),
        out_specs=P("mrow", "mcol"),
        check_vma=False,
    )
```
